256 devices in a mesh: rep: 16 (over z, x_hi), shard: 16 (over y, x_lo, core).
Axes of the slice: x: 4 (x_hi: 2, x_lo: 2; x = x_hi * 2 + x_lo), y: 4, z: 8, core: 2. Of those that a mesh axis runs over, the one named last changes fastest.
Arguments:
- tokens: bfloat16 [32768, 2048], P(('rep', 'shard')), may hold values from -6 to 6
- norm_gain: bfloat16 [2048], replicated, may hold values from 0.099609375 to 1.8984375
- cotangent: bfloat16 [32768, 8192], P(('rep', 'shard')), may hold values from -24 to 24
- token_ids: int32 [32768], P(('rep', 'shard')), may hold values from 0 to 31999, as said below
- step_index: int32 [1], replicated, may hold values from 0 to 1023
- block_rows: int32 [64, 4], replicated, may hold values from 0 to 15, as said below
- weights: bfloat16 [16, 64, 4, 128, 128], P('rep', 'shard'), may hold values from -6 to 6
- momentum: bfloat16 [16, 64, 4, 128, 128], P('rep', 'shard'), may hold values from -4 to 4
Outputs:
- grad_tokens: bfloat16 [32768, 2048], P(('rep', 'shard'))
- new_weights: bfloat16 [16, 64, 4, 128, 128], P('rep', 'shard')
- new_momentum: bfloat16 [16, 64, 4, 128, 128], P('rep', 'shard')
The draws below stay inside these ranges and needn't reach their ends.
Inputs may be any that keep to these rules, and one draw needn't show every extreme that they name: `block_rows`: each row names 4 different blocks of features. `token_ids`: 0 marks padding; in each sequence of 2048 consecutive tokens the padding follows all other tokens and takes 1 to 1024 positions; the first token of every sequence is 31999.
All inputs are finite; a program needn't handle non-finite values.
Results may differ from the reference program's by a relative error of at most 0.02.
Values may be sent and summed in bfloat16 or wider, within the bound.
No kernel may reach another device: no remote copies, remote signals or barrier semaphores. Data moves between devices by JAX's collectives and lax.ppermute only.
A program may use at most 128 MiB of HBM per device.

```python
from functools import partial
import jax
import jax.numpy as jnp
from jax import lax

BLK = 128
D = 2048
FF = 8192
VOCAB = 32000
TOK_DEV = 128
DB = 16
FB = 64
KB = 4
SEQ = 2048
TOKENS = 32768
N_REP = 16
N_SHARD = 16


def draw_block_rows(key, part):
    key = jax.random.fold_in(key, 11)
    column_keys = jax.random.split(key, FB)
    shuffled = jax.vmap(lambda subkey: jax.random.permutation(subkey, DB))(column_keys)
    return shuffled[:, :KB].astype(jnp.int32)


def draw_token_ids(key, part):
    key = jax.random.fold_in(key, 23)
    key_ids, key_lengths = jax.random.split(key)
    sequences = TOKENS // SEQ
    raw_ids = jax.random.randint(key_ids, (sequences, SEQ), 1, VOCAB)
    position = jnp.arange(SEQ)[None, :]
    raw_ids = jnp.where(position == 0, VOCAB - 1, raw_ids)
    lengths = jax.random.randint(key_lengths, (sequences, 1), SEQ // 2, SEQ)
    return jnp.where(position < lengths, raw_ids, 0).reshape(TOKENS).astype(jnp.int32)


def raised(drawn, rng, source, target, parts, factor):
    owner, partner = [(jnp.arange(drawn.shape[dim]) // (drawn.shape[dim] // parts)).reshape([-1 if axis == dim else 1 for axis in range(drawn.ndim)]) for dim in (source, target)]
    chosen = jax.random.permutation(rng, parts)[partner]
    strong = (owner == chosen) | (owner == (partner + parts // 2) % parts)
    return jnp.where(strong, factor * drawn, drawn)


def level_of(stream_key, extent, shards, least, largest):
    factor_of = 1.0
    for dim, blocks in shards:
        steps = jax.random.uniform(jax.random.fold_in(jax.random.fold_in(stream_key, 6), dim), (blocks,), jnp.float32, least / len(shards), largest / len(shards))
        factor_of = factor_of * jnp.repeat(jnp.exp(steps), extent[dim] // blocks).reshape((-1,) + (1,) * (len(extent) - 1 - dim))
    return factor_of


def scatter_about(rng, shape, spread, reach, cuts=(), kind=jnp.bfloat16):
    entries = spread * jax.random.normal(rng, shape, jnp.float32)
    if cuts:
        entries = entries * level_of(rng, shape, cuts, -0.22, 0.18)
    return jnp.clip(entries, -reach, reach).astype(kind)


def noise_with(stream_key, extent, deviation, reach, pieces, heavy, dtype=jnp.bfloat16):
    result = deviation * jax.random.normal(stream_key, extent, jnp.float32)
    if pieces:
        result = result * level_of(stream_key, extent, pieces, -0.22, 0.18)
    return jnp.clip(raised(result, jax.random.fold_in(stream_key, 3), *heavy), -reach, reach).astype(dtype)


def setup_inputs(seed: int = 0) -> dict:
    key_list = jax.random.split(jax.random.key(seed), 9)
    return {
        "tokens": scatter_about(key_list[0], (TOKENS, D), 1.0, 6.0, ((0, 256),)),
        "norm_gain": jnp.clip(1.0 + 0.18 * jax.random.normal(key_list[1], (D,), jnp.float32), 0.099609375, 1.8984375).astype(jnp.bfloat16),
        "cotangent": noise_with(key_list[2], (TOKENS, FF), 1.0, 24.0, ((0, 256),), (0, 1, 256, 6.0)),
        "token_ids": draw_token_ids(jax.random.fold_in(key_list[8], 71), 0),
        "step_index": jax.random.randint(key_list[4], (1,), 0, 1024).astype(jnp.int32),
        "block_rows": draw_block_rows(jax.random.fold_in(key_list[8], 71), 0),
        "weights": scatter_about(key_list[6], (N_REP, FB, KB, BLK, BLK), 1.0, 6.0, ((0, 16), (1, 16))),
        "momentum": scatter_about(key_list[7], (N_REP, FB, KB, BLK, BLK), 0.5, 4.0, ((0, 16), (1, 16))),
    }


def silu_slope(preact):
    sigmoid_val = jax.nn.sigmoid(preact)
    return sigmoid_val * (1.0 + preact * (1.0 - sigmoid_val))

def replica_step(norm_gain, block_rows, inputs):
    tokens, cotangent, token_ids, weights, momentum, partner_weights, partner_moment = inputs
    fan_scale = float(KB * BLK) ** (-0.5)
    wide_tokens = tokens.astype(jnp.float32)
    inv_rms = lax.rsqrt(lax.optimization_barrier(jnp.mean(wide_tokens * wide_tokens, axis=1, keepdims=True)) + 1e-05)
    gain_row = norm_gain.astype(jnp.float32)[None, :]
    normed = (wide_tokens * inv_rms * gain_row).astype(jnp.bfloat16)
    normed_blocks = normed.reshape(-1, DB, BLK)
    wide_weights = weights.astype(jnp.float32)
    preact = jnp.zeros((normed.shape[0], FB, BLK), jnp.float32)
    for slot_index in range(KB):
        picked = normed_blocks[:, block_rows[:, slot_index]].astype(jnp.float32)
        preact = preact + jnp.einsum('tpb,pbc->tpc', picked, wide_weights[:, slot_index])
    preact = preact * fan_scale
    live_mask = (token_ids != 0).astype(jnp.float32)[:, None, None]
    grad_pre = (cotangent.astype(jnp.float32).reshape(-1, FB, BLK) * live_mask * silu_slope(preact)).astype(jnp.bfloat16)
    normed_shards = normed_blocks.reshape(N_SHARD, TOK_DEV, DB, BLK)
    grad_shards = grad_pre.reshape(N_SHARD, TOK_DEV, FB, BLK)

    def add_shard(running, shard_pair):
        normed_dev, grad_dev = shard_pair
        columns = grad_dev.astype(jnp.float32)
        partials = [jnp.einsum('tpb,tpc->pbc', normed_dev[:, block_rows[:, slot_index]].astype(jnp.float32), columns) for slot_index in range(KB)]
        rounded = (jnp.stack(partials, axis=1) * fan_scale).astype(jnp.bfloat16)
        rounded = lax.optimization_barrier(rounded)
        return (running + rounded.astype(jnp.float32), None)
    weight_grad, _ = lax.scan(add_shard, jnp.zeros((FB, KB, BLK, BLK), jnp.float32), (normed_shards, grad_shards))
    grad_normed = jnp.zeros((normed.shape[0], DB, BLK), jnp.float32)
    grad_wide = grad_pre.astype(jnp.float32)
    for slot_index in range(KB):
        contrib = jnp.einsum('tpc,pbc->tpb', grad_wide, wide_weights[:, slot_index])
        grad_normed = grad_normed.at[:, block_rows[:, slot_index]].add(contrib)
    grad_normed = (grad_normed * fan_scale).reshape(-1, D)
    gain_grad = gain_row * grad_normed
    grad_tokens = inv_rms * gain_grad - wide_tokens * inv_rms ** 3 * lax.optimization_barrier(jnp.mean(wide_tokens * gain_grad, axis=1, keepdims=True))
    mean_weights = (weights.astype(jnp.float32) + partner_weights.astype(jnp.float32)) * 0.5
    mean_moment = (momentum.astype(jnp.float32) + partner_moment.astype(jnp.float32)) * 0.5
    moment_sum = 0.9 * mean_moment + weight_grad
    new_weights = mean_weights - 0.05 * moment_sum
    return (grad_tokens.astype(jnp.bfloat16), new_weights.astype(jnp.bfloat16), moment_sum.astype(jnp.bfloat16))

def reference(tokens, norm_gain, cotangent, token_ids, step_index, block_rows, weights, momentum):
    replica_rows = TOK_DEV * N_SHARD
    levels = N_REP.bit_length() - 1
    distance = jnp.left_shift(jnp.int32(1), step_index[0] % levels)
    partner_weights = jnp.roll(weights, distance, axis=0)
    partner_moment = jnp.roll(momentum, distance, axis=0)
    inputs = (tokens.reshape(N_REP, replica_rows, D), cotangent.reshape(N_REP, replica_rows, FF), token_ids.reshape(N_REP, replica_rows), weights, momentum, partner_weights, partner_moment)
    grad_tokens, new_weights, new_momentum = lax.map(partial(replica_step, norm_gain, block_rows), inputs)
    return (grad_tokens.reshape(TOKENS, D), new_weights, new_momentum)
```

```python
import functools

import jax
import jax.numpy as jnp
from jax import lax
from jax.experimental import pallas as pl
from jax.experimental.pallas import tpu as pltpu
from jax.sharding import PartitionSpec as P

B = 128
EPS = 1e-05
MIB = 1 << 20
VMEM = pl.BlockSpec(memory_space=pltpu.VMEM)
SMEM = pl.BlockSpec(memory_space=pltpu.SMEM)


def call(body, out, args, n_smem=0, scratch=(), flops=0, limit=24):
    moved = sum(a.size * a.dtype.itemsize for a in args[n_smem:])
    moved += sum(o.size * o.dtype.itemsize for o in out)
    return pl.pallas_call(
        body,
        out_shape=tuple(out),
        in_specs=[SMEM] * n_smem + [VMEM] * (len(args) - n_smem),
        out_specs=tuple(VMEM for _ in out),
        scratch_shapes=list(scratch),
        compiler_params=pltpu.CompilerParams(vmem_limit_bytes=limit * MIB),
        cost_estimate=pl.CostEstimate(flops=flops, bytes_accessed=moved, transcendentals=0),
    )(*args)


def shaped(shape, dtype=jnp.bfloat16):
    return jax.ShapeDtypeStruct(shape, dtype)


def pack_body(offsets, ids, cot, *outs):
    mask = jnp.where(ids[...] != 0, 1.0, 0.0).astype(jnp.float32)
    wide = jnp.broadcast_to(mask, (B, B))
    for d in range(len(outs)):
        for i in range(outs[d].shape[0]):
            column = pl.multiple_of(offsets[d, i] * B, B)
            outs[d][i] = (cot[:, pl.ds(column, B)].astype(jnp.float32) * wide).astype(jnp.bfloat16)


def norm_body(gain, *refs):
    count = (len(refs) - 2)
    normed, turned = refs[count:]
    blocks = normed.shape[0]
    for t in range(count):
        tok = refs[t]
        total = jnp.zeros((B, B), jnp.float32)
        for f in range(blocks):
            part = tok[:, f * B : (f + 1) * B].astype(jnp.float32)
            total = total + part * part
        mean = jnp.sum(total, axis=1, keepdims=True) * (1.0 / (blocks * B))
        inv = lax.rsqrt(mean + EPS)
        for f in range(blocks):
            part = tok[:, f * B : (f + 1) * B].astype(jnp.float32)
            scaled = part * inv * gain[:, f * B : (f + 1) * B].astype(jnp.float32)
            normed[f, t * B : (t + 1) * B, :] = scaled.astype(jnp.bfloat16)
            turned[f, :, t * B : (t + 1) * B] = scaled.T.astype(jnp.bfloat16)


def picked(ref, rows, j):
    return [ref[rows[j, m]] for m in range(rows.shape[1])]


def forward_block(rows, normed, cots, weight, j, i, scale):
    left = jnp.concatenate(picked(normed, rows, j), axis=1)
    pre = jnp.dot(left, weight, preferred_element_type=jnp.float32) * scale
    cot = jnp.concatenate([c[i] for c in cots], axis=0).astype(jnp.float32)
    sig = jax.nn.sigmoid(pre)
    return (cot * (sig * (1.0 + pre * (1.0 - sig)))).astype(jnp.bfloat16)


def back_block(rows, acc, grad, weight, j):
    out = lax.dot_general(grad, weight, (((1,), (1,)), ((), ())), preferred_element_type=jnp.float32)
    for m in range(rows.shape[1]):
        f = rows[j, m]
        acc[f] = acc[f] + out[:, m * B : (m + 1) * B]


def near_body(scale, rows, normed, c0a, c1a, c0b, c1b, w0, w2, w1, w3, grads, mine, theirs, acc):
    acc[...] = jnp.zeros_like(acc)
    per = w0.shape[0]
    for g, (weights, cots) in enumerate(
        ((w0, (c0a, c1a)), (w2, (c0a, c1a)), (w1, (c0b, c1b)), (w3, (c0b, c1b)))
    ):

        def step(r, _, g=g, weights=weights, cots=cots):
            j = g * per + r
            weight = weights[r]
            grad = forward_block(rows, normed, cots, weight, j, (g % 2) * per + r, scale)
            grads[j] = grad
            back_block(rows, acc, grad, weight, j)
            return 0

        lax.fori_loop(0, per, step, 0)
    mine[...] = acc[:, :B, :] * scale
    theirs[...] = (acc[:, B:, :] * scale).astype(jnp.bfloat16)


def far_first_body(scale, rows, normed, c2, c3, w0, w2, grads):
    per = w0.shape[0]
    for g, weights in enumerate((w0, w2)):

        def step(r, _, g=g, weights=weights):
            j = g * per + r
            grads[j] = forward_block(rows, normed, (c2, c3), weights[r], j, j, scale)
            return 0

        lax.fori_loop(0, per, step, 0)


def far_second_body(scale, rows, normed, c2, c3, first, w0, w2, w1, w3, grads, kept, passed, acc):
    acc[...] = jnp.zeros_like(acc)
    per = w0.shape[0]
    for g, weights in enumerate((w0, w2, w1, w3)):

        def step(r, _, g=g, weights=weights):
            j = g * per + r
            weight = weights[r]
            if g < 2:
                grad = first[j]
            else:
                i = j - 2 * per
                grad = forward_block(rows, normed, (c2, c3), weight, j, i, scale)
                grads[i] = grad
            back_block(rows, acc, grad, weight, j)
            return 0

        lax.fori_loop(0, per, step, 0)
    kept[...] = acc[:, :B, :] * scale
    passed[...] = (acc[:, B:, :] * scale).astype(jnp.bfloat16)


def weight_body(scale, base, rows, near_turned, far_turned, near_grads, far_grads, out_a, out_b):
    per = out_a.shape[0]
    for g, out in enumerate((out_a, out_b)):

        def step(r, _, g=g, out=out):
            i = g * per + r
            j = base + i
            near = jnp.concatenate(picked(near_turned, rows, j), axis=0)
            far = jnp.concatenate(picked(far_turned, rows, j), axis=0)
            total = jnp.dot(near, near_grads[j], preferred_element_type=jnp.float32)
            total = total + jnp.dot(far, far_grads[i], preferred_element_type=jnp.float32)
            out[r] = (total * scale).astype(jnp.bfloat16)
            return 0

        lax.fori_loop(0, per, step, 0)


def final_body(gain, tok, mine, core_part, far_part, out):
    blocks = mine.shape[0]
    total = jnp.zeros((B, B), jnp.float32)
    cross = jnp.zeros((B, B), jnp.float32)
    for f in range(blocks):
        part = tok[:, f * B : (f + 1) * B].astype(jnp.float32)
        total = total + part * part
        grad = mine[f] + core_part[f].astype(jnp.float32) + far_part[f].astype(jnp.float32)
        grad = grad * gain[:, f * B : (f + 1) * B].astype(jnp.float32)
        mine[f] = grad
        cross = cross + part * grad
    inv = lax.rsqrt(jnp.sum(total, axis=1, keepdims=True) * (1.0 / (blocks * B)) + EPS)
    mean = jnp.sum(cross, axis=1, keepdims=True) * (1.0 / (blocks * B))
    slope = inv * inv * inv * mean
    for f in range(blocks):
        part = tok[:, f * B : (f + 1) * B].astype(jnp.float32)
        out[:, f * B : (f + 1) * B] = (inv * mine[f] - part * slope).astype(jnp.bfloat16)


def final_entry(gain, tok, mine, core_part, far_part, out, kept):
    kept[...] = mine[...]
    final_body(gain, tok, kept, core_part, far_part, out)


def branch(exponent, tokens, gain, cotangent, ids, block_rows, weights, momentum):
    blocks = tokens.shape[1] // B
    per, slots = weights.shape[0], weights.shape[1]
    scale = float(slots * B) ** -0.5
    size = lax.axis_size("shard")
    ring = size // 4
    me = lax.axis_index("shard")
    y, q = me // 4, me % 4

    def hop(value, flip):
        return lax.ppermute(value, "shard", [(s, s ^ flip) for s in range(size)])

    def along(value, steps):
        return lax.ppermute(value, "shard", [(s, (s + 4 * steps) % size) for s in range(size)])

    def rep(value):
        count = lax.axis_size("rep")
        return lax.ppermute(value, "rep", [(s, (s + 2**exponent) % count) for s in range(count)])

    order = (0, 2, 1, 3)
    owners = jnp.stack([(y + dy) % ring for dy in order])
    first = (owners[:, None] * (4 * per) + jnp.arange(per)[None, :]).reshape(-1)
    half = 2 * per
    listed = first + q * per
    pieces = jnp.stack([first + (q ^ d) * per for d in range(4)])
    offsets_far = jnp.stack([pieces[2, :half], pieces[3, :half], pieces[2, half:], pieces[3, half:]])
    offsets_near = jnp.stack([pieces[0, :half], pieces[0, half:], pieces[1, :half], pieces[1, half:]])
    rows = jnp.sum(
        jnp.where(jnp.arange(block_rows.shape[0])[None, :, None] == listed[:, None, None], block_rows[None], 0),
        axis=1,
    )

    tok_far = hop(tokens, 2)
    part = shaped((half, B, B))
    c2a, c3a, c2b, c3b = call(pack_body, [part] * 4, (offsets_far, ids, cotangent), n_smem=1)
    c2a, c3a = hop(c2a, 2), hop(c3a, 3)
    c2b, c3b = hop(c2b, 2), hop(c3b, 3)
    w = {0: weights}
    for dy in (2, 1, 3):
        w[dy] = along(weights, -dy)
    partner_w, partner_m = rep(weights), rep(momentum)
    tok_core = hop(tokens, 1)
    c0a, c0b, c1a, c1b = call(pack_body, [part] * 4, (offsets_near, ids, cotangent), n_smem=1)
    c1a, c1b = hop(c1a, 1), hop(c1b, 1)
    tok_diag = hop(tok_far, 1)

    flat = {dy: w[dy].reshape(per, slots * B, B) for dy in w}
    both = [shaped((blocks, 2 * B, B)), shaped((blocks, B, 2 * B))]
    near, near_turned = call(norm_body, both, (gain, tokens, tok_core))
    far, far_turned = call(norm_body, both, (gain, tok_far, tok_diag))
    acc = pltpu.VMEM((blocks, 2 * B, B), jnp.float32)
    unit = 2 * 2 * B * half * slots * B * B
    near_grads, mine, theirs = call(
        functools.partial(near_body, scale),
        [shaped((2 * half, 2 * B, B)), shaped((blocks, B, B), jnp.float32), shaped((blocks, B, B))],
        (rows, near, c0a, c1a, c0b, c1b, flat[0], flat[2], flat[1], flat[3]),
        n_smem=1,
        scratch=[acc],
        flops=4 * unit,
    )
    core_part = hop(theirs, 1)
    (far_a,) = call(
        functools.partial(far_first_body, scale),
        [shaped((half, 2 * B, B))],
        (rows, far, c2a, c3a, flat[0], flat[2]),
        n_smem=1,
        flops=unit,
    )
    terms = [shaped((per, slots * B, B))] * 2
    g0, g2 = call(
        functools.partial(weight_body, scale, 0),
        terms,
        (rows, near_turned, far_turned, near_grads, far_a),
        n_smem=1,
        flops=2 * unit,
    )
    got2 = along(g2, 2)
    far_b, kept, passed = call(
        functools.partial(far_second_body, scale),
        [shaped((half, 2 * B, B)), shaped((blocks, B, B), jnp.float32), shaped((blocks, B, B))],
        (rows, far, c2b, c3b, far_a, flat[0], flat[2], flat[1], flat[3]),
        n_smem=1,
        scratch=[acc],
        flops=3 * unit,
    )
    far_part = hop((kept + hop(passed, 1).astype(jnp.float32)).astype(jnp.bfloat16), 2)
    g1, g3 = call(
        functools.partial(weight_body, scale, half),
        terms,
        (rows, near_turned, far_turned, near_grads, far_b),
        n_smem=1,
        flops=2 * unit,
    )
    got1, got3 = along(g1, 1), along(g3, 3)

    (grad_tokens,) = call(
        final_entry,
        [shaped(tokens.shape)],
        (gain, tokens, mine, core_part, far_part),
        scratch=[pltpu.VMEM((blocks, B, B), jnp.float32)],
    )
    shape = weights.shape
    weight_grad = sum(g.reshape(shape).astype(jnp.float32) for g in (g0, got1, got2, got3))
    f32 = jnp.float32
    mean_weights = (weights.astype(f32) + partner_w.astype(f32)) * 0.5
    mean_moment = (momentum.astype(f32) + partner_m.astype(f32)) * 0.5
    moment_sum = 0.9 * mean_moment + weight_grad
    new_weights = (mean_weights - 0.05 * moment_sum).astype(jnp.bfloat16)
    return grad_tokens, new_weights, moment_sum.astype(jnp.bfloat16)


def per_device(tokens, norm_gain, cotangent, token_ids, step_index, block_rows, weights, momentum):
    levels = lax.axis_size("rep").bit_length() - 1
    grad_tokens, new_weights, new_momentum = lax.switch(
        step_index[0] % levels,
        [functools.partial(branch, e) for e in range(levels)],
        tokens,
        norm_gain[None, :],
        cotangent,
        token_ids[:, None],
        block_rows,
        weights[0],
        momentum[0],
    )
    return grad_tokens, new_weights[None], new_momentum[None]


def solution(mesh):
    placed = (
        P(("rep", "shard"), None),
        P(),
        P(("rep", "shard"), None),
        P(("rep", "shard")),
        P(),
        P(),
        P("rep", "shard", None, None, None),
        P("rep", "shard", None, None, None),
    )
    return jax.shard_map(
        per_device,
        mesh=mesh,
        in_specs=placed,
        out_specs=(
            P(("rep", "shard"), None),
            P("rep", "shard", None, None, None),
            P("rep", "shard", None, None, None),
        ),
        check_vma=False,
    )
```

```python
import functools

import jax
import jax.numpy as jnp
from jax import lax
from jax.experimental import pallas as pl
from jax.experimental.pallas import tpu as pltpu
from jax.sharding import PartitionSpec as P

B = 128
EPS = 1e-05
MIB = 1 << 20
VMEM = pl.BlockSpec(memory_space=pltpu.VMEM)
SMEM = pl.BlockSpec(memory_space=pltpu.SMEM)


def call(body, out, args, n_smem=0, scratch=(), limit=60, moved=0):
    return pl.pallas_call(
        body,
        out_shape=tuple(out),
        in_specs=[SMEM] * n_smem + [VMEM] * (len(args) - n_smem),
        out_specs=tuple(VMEM for _ in out),
        scratch_shapes=list(scratch),
        compiler_params=pltpu.CompilerParams(vmem_limit_bytes=limit * MIB),
        cost_estimate=pl.CostEstimate(flops=0, bytes_accessed=moved, transcendentals=0),
    )(*args)


def shaped(shape, dtype=jnp.bfloat16):
    return jax.ShapeDtypeStruct(shape, dtype)


def pack_body(offsets, ids, cot, *outs):
    mask = jnp.where(ids[...] != 0, 1.0, 0.0).astype(jnp.float32)
    wide = jnp.broadcast_to(mask, (B, B))
    d_of = (0, 1, 2, 2, 3, 3)
    for out, d, start in zip(outs, d_of, (0, 0, 0, outs[2].shape[0], 0, outs[2].shape[0])):
        for i in range(out.shape[0]):
            column = pl.multiple_of(offsets[d, start + i] * B, B)
            out[i] = (cot[:, pl.ds(column, B)].astype(jnp.float32) * wide).astype(jnp.bfloat16)


def norm_body(gain, *refs):
    count = (len(refs) - 2)
    normed, turned = refs[count:]
    blocks = normed.shape[0]
    for t in range(count):
        tok = refs[t]
        total = jnp.zeros((B, B), jnp.float32)
        for f in range(blocks):
            part = tok[:, f * B : (f + 1) * B].astype(jnp.float32)
            total = total + part * part
        mean = jnp.sum(total, axis=1, keepdims=True) * (1.0 / (blocks * B))
        inv = lax.rsqrt(mean + EPS)
        for f in range(blocks):
            part = tok[:, f * B : (f + 1) * B].astype(jnp.float32)
            scaled = part * inv * gain[:, f * B : (f + 1) * B].astype(jnp.float32)
            normed[f, t * B : (t + 1) * B, :] = scaled.astype(jnp.bfloat16)
            turned[f, :, t * B : (t + 1) * B] = scaled.T.astype(jnp.bfloat16)


def merge_body(own, got, out):
    count = own.shape[0]
    out[:count] = own[...]
    out[count:] = got[...]


class Rows:
    def __init__(self, lists, offsets):
        self.lists, self.offsets, self.slots = lists, offsets, lists.shape[0]

    def __getitem__(self, jm):
        j, m = jm
        return self.lists[m, self.offsets[0, j]]


def picked(ref, rows, j):
    return [ref[rows[j, m]] for m in range(rows.slots)]


def forward_block(rows, normed, cots, weight, j, scale):
    left = jnp.concatenate(picked(normed, rows, j), axis=1)
    pre = jnp.dot(left, weight, preferred_element_type=jnp.float32) * scale
    cot = jnp.concatenate(cots, axis=0).astype(jnp.float32)
    sig = jax.nn.sigmoid(pre)
    return (cot * (sig * (1.0 + pre * (1.0 - sig)))).astype(jnp.bfloat16)


def back_block(rows, acc, grad, weight, j):
    out = lax.dot_general(grad, weight, (((1,), (1,)), ((), ())), preferred_element_type=jnp.float32)
    for m in range(rows.slots):
        f = rows[j, m]
        acc[f] = acc[f] + out[:, m * B : (m + 1) * B]


def near_body(scale, lists, offsets, normed, own, got, w0, w2, w1, w3, grads, mine, theirs, acc):
    acc[...] = jnp.zeros_like(acc)
    rows = Rows(lists, offsets)
    per = w0.shape[0]

    def step(r, _):
        done = []
        for g, weights in enumerate((w0, w2, w1, w3)):
            j = g * per + r
            grad = forward_block(rows, normed, (own[j], got[j]), weights[r], j, scale)
            grads[j] = grad
            done.append((grad, weights, j))
        for grad, weights, j in done:
            back_block(rows, acc, grad, weights[r], j)
        return 0

    lax.fori_loop(0, per, step, 0)
    mine[...] = acc[:, :B, :] * scale
    theirs[...] = (acc[:, B:, :] * scale).astype(jnp.bfloat16)


def far_steps(scale, base, rows, normed, cots, pair, grads, acc):
    per = pair[0].shape[0]
    half = 2 * per

    def step(r, _):
        done = []
        for g, weights in enumerate(pair):
            i = g * per + r
            grad = forward_block(rows, normed, (cots[i], cots[half + i]), weights[r], base + i, scale)
            grads[i] = grad
            done.append((grad, weights, base + i))
        for grad, weights, j in done:
            back_block(rows, acc, grad, weights[r], j)
        return 0

    lax.fori_loop(0, per, step, 0)


def far_first_body(scale, lists, offsets, normed, cots, w0, w2, grads, acc):
    acc[...] = jnp.zeros_like(acc)
    far_steps(scale, 0, Rows(lists, offsets), normed, cots, (w0, w2), grads, acc)


def far_second_body(scale, base, lists, offsets, normed, cots, before, w1, w3, grads, kept, passed, acc):
    acc[...] = before[...]
    far_steps(scale, base, Rows(lists, offsets), normed, cots, (w1, w3), grads, acc)
    kept[...] = acc[:, :B, :] * scale
    passed[...] = (acc[:, B:, :] * scale).astype(jnp.bfloat16)


def weight_body(scale, base, lists, offsets, near_turned, far_turned, near_grads, far_grads, out_a, out_b):
    per = out_a.shape[0]
    rows = Rows(lists, offsets)

    def step(r, _):
        for g, out in enumerate((out_a, out_b)):
            i = g * per + r
            j = base + i
            near = jnp.concatenate(picked(near_turned, rows, j), axis=0)
            far = jnp.concatenate(picked(far_turned, rows, j), axis=0)
            total = jnp.dot(near, near_grads[j], preferred_element_type=jnp.float32)
            total = total + jnp.dot(far, far_grads[i], preferred_element_type=jnp.float32)
            out[r] = (total * scale).astype(jnp.bfloat16)
        return 0

    lax.fori_loop(0, per, step, 0)


def sum_body(kept, passed, out):
    out[...] = (kept[...] + passed[...].astype(jnp.float32)).astype(jnp.bfloat16)


def final_body(gain, tok, mine, core_part, far_part, out):
    blocks = mine.shape[0]
    total = jnp.zeros((B, B), jnp.float32)
    cross = jnp.zeros((B, B), jnp.float32)
    for f in range(blocks):
        part = tok[:, f * B : (f + 1) * B].astype(jnp.float32)
        total = total + part * part
        grad = mine[f] + core_part[f].astype(jnp.float32) + far_part[f].astype(jnp.float32)
        grad = grad * gain[:, f * B : (f + 1) * B].astype(jnp.float32)
        mine[f] = grad
        cross = cross + part * grad
    inv = lax.rsqrt(jnp.sum(total, axis=1, keepdims=True) * (1.0 / (blocks * B)) + EPS)
    mean = jnp.sum(cross, axis=1, keepdims=True) * (1.0 / (blocks * B))
    slope = inv * inv * inv * mean
    for f in range(blocks):
        part = tok[:, f * B : (f + 1) * B].astype(jnp.float32)
        out[:, f * B : (f + 1) * B] = (inv * mine[f] - part * slope).astype(jnp.bfloat16)


def final_entry(gain, tok, mine, core_part, far_part, out, kept):
    kept[...] = mine[...]
    final_body(gain, tok, kept, core_part, far_part, out)


def after(value, *earlier):
    return lax.optimization_barrier((value, earlier))[0]


def grouped(valid, work, *values):
    shapes = jax.eval_shape(work, *values)
    empty = lambda *_: jax.tree.map(lambda a: jnp.zeros(a.shape, a.dtype), shapes)
    return lax.cond(valid, work, empty, *values)


def per_device(tokens, norm_gain, cotangent, token_ids, step_index, block_rows, weights, momentum):
    gain, ids = norm_gain[None, :], token_ids[:, None]
    weights, momentum = weights[0], momentum[0]
    blocks = tokens.shape[1] // B
    per, slots = weights.shape[0], weights.shape[1]
    scale = float(slots * B) ** -0.5
    size = lax.axis_size("shard")
    ring = size // 4
    me = lax.axis_index("shard")
    y, q = me // 4, me % 4
    count = lax.axis_size("rep")
    levels = count.bit_length() - 1

    def hop(value, flip):
        return lax.ppermute(value, "shard", [(s, s ^ flip) for s in range(size)])

    def along(value, steps):
        return lax.ppermute(value, "shard", [(s, (s + 4 * steps) % size) for s in range(size)])

    def rep(exponent, value):
        return lax.ppermute(value, "rep", [(s, (s + 2**exponent) % count) for s in range(count)])

    def partner(value):
        return lax.switch(step_index[0] % levels, [functools.partial(rep, e) for e in range(levels)], value)

    order = (0, 2, 1, 3)
    owners = jnp.stack([(y + dy) % ring for dy in order])
    first = (owners[:, None] * (4 * per) + jnp.arange(per)[None, :]).reshape(-1)
    half = 2 * per
    full = 2 * half
    offsets = jnp.stack([first + (q ^ d) * per for d in range(4)])
    lists = block_rows.T
    acc = shaped((blocks, 2 * B, B), jnp.float32)
    scratch = [pltpu.VMEM(acc.shape, acc.dtype)]
    sums = [shaped((blocks, B, B), jnp.float32), shaped((blocks, B, B))]
    both = [shaped((blocks, 2 * B, B)), shaped((blocks, B, 2 * B))]
    terms = [shaped((per, slots * B, B))] * 2
    grads = shaped((half, 2 * B, B))
    piece = shaped((full, B, B))

    part = shaped((half, B, B))
    valid = step_index[0] >= 0

    def opening(tokens, cotangent):
        tok_core = hop(tokens, 1)
        own, for_core, near_a, near_b, far_a, far_b = call(
            pack_body, [piece, piece, part, part, part, part], (offsets, ids, cotangent), n_smem=1
        )
        far_a, far_b = after((far_a, far_b), tok_core)
        got_a, got_b = hop(far_a, 1), hop(far_b, 1)
        got = hop(after(for_core, (got_a, got_b)), 1)
        (send_a,) = call(merge_body, [piece], (near_a, got_a))
        (send_b,) = call(merge_body, [piece], (near_b, got_b))
        near, near_turned = call(norm_body, both, (gain, tokens, tok_core))
        return own, got, send_a, send_b, near, near_turned

    tok_far = hop(tokens, 2)
    w1, w3 = along(weights, -1), along(weights, -3)
    own, got, send_a, send_b, near, near_turned = grouped(valid, opening, tokens, cotangent)
    tok_far, w1, w3 = after((tok_far, w1, w3), near)
    w2 = along(after(weights, (w1, w3)), -2)
    tok_diag = hop(after(tok_far, (w1, w3)), 1)
    far_cots_a = hop(send_a, 2)
    far_cots_b = hop(after(send_b, (tok_far, w1, w3)), 2)
    far, far_turned = call(norm_body, both, (gain, tok_far, tok_diag))

    partner_w = partner(after(weights, (far, tok_diag)))
    flat = [v.reshape(per, slots * B, B) for v in (weights, w2, w1, w3)]
    near_grads, mine, theirs = call(
        functools.partial(near_body, scale),
        [shaped((full, 2 * B, B)), *sums],
        (lists, offsets, after(near, partner_w), own, got, *flat),
        n_smem=2,
        scratch=scratch,
    )
    core_part = hop(theirs, 1)
    far_a, running = call(
        functools.partial(far_first_body, scale),
        [grads, acc],
        (lists, offsets, after(far, near_grads), far_cots_a, *flat[:2]),
        n_smem=2,
    )
    g0, g2 = call(
        functools.partial(weight_body, scale, 0),
        terms,
        (lists, offsets, near_turned, far_turned, near_grads, far_a),
        n_smem=2,
    )
    got2 = along(g2, 2)
    far_b, kept, passed = call(
        functools.partial(far_second_body, scale, half),
        [grads, *sums],
        (lists, offsets, after(far, (g0, core_part)), far_cots_b, running, *flat[2:]),
        n_smem=2,
        scratch=scratch,
    )

    def total(kept, passed):
        return call(sum_body, [shaped(kept.shape)], (kept, hop(passed, 1)))[0]

    summed = grouped(valid, total, kept, passed)
    far_part = hop(summed, 2)
    g1, g3 = call(
        functools.partial(weight_body, scale, half),
        terms,
        (lists, offsets, near_turned, far_turned, after(near_grads, summed), far_b),
        n_smem=2,
    )
    got1, got3 = along(g1, 1), along(g3, 3)
    partner_m = partner(after(momentum, (summed, g1, g3)))
    far_part, got2 = after((far_part, got2), partner_m)

    (grad_tokens,) = call(
        final_entry,
        [shaped(tokens.shape)],
        (gain, after(tokens, got2), mine, core_part, far_part),
        moved=20 * MIB,
        scratch=[pltpu.VMEM((blocks, B, B), jnp.float32)],
    )
    got1, got3 = after((got1, got3), grad_tokens)
    shape = weights.shape
    weight_grad = sum(g.reshape(shape).astype(jnp.float32) for g in (g0, got1, got2, got3))
    f32 = jnp.float32
    mean_weights = (weights.astype(f32) + partner_w.astype(f32)) * 0.5
    mean_moment = (momentum.astype(f32) + partner_m.astype(f32)) * 0.5
    moment_sum = 0.9 * mean_moment + weight_grad
    new_weights = (mean_weights - 0.05 * moment_sum).astype(jnp.bfloat16)
    return grad_tokens, new_weights[None], moment_sum.astype(jnp.bfloat16)[None]


def solution(mesh):
    placed = (
        P(("rep", "shard"), None),
        P(),
        P(("rep", "shard"), None),
        P(("rep", "shard")),
        P(),
        P(),
        P("rep", "shard", None, None, None),
        P("rep", "shard", None, None, None),
    )
    return jax.shard_map(
        per_device,
        mesh=mesh,
        in_specs=placed,
        out_specs=(
            P(("rep", "shard"), None),
            P("rep", "shard", None, None, None),
            P("rep", "shard", None, None, None),
        ),
        check_vma=False,
    )
```

```python
import functools

import jax
import jax.numpy as jnp
from jax import lax
from jax.experimental import pallas as pl
from jax.experimental.pallas import tpu as pltpu
from jax.sharding import PartitionSpec as P

B = 128
EPS = 1e-05
MIB = 1 << 20
VMEM = pl.BlockSpec(memory_space=pltpu.VMEM)
SMEM = pl.BlockSpec(memory_space=pltpu.SMEM)


def call(body, out, args, n_smem=0, scratch=(), limit=60, moved=0):
    return pl.pallas_call(
        body,
        out_shape=tuple(out),
        in_specs=[SMEM] * n_smem + [VMEM] * (len(args) - n_smem),
        out_specs=tuple(VMEM for _ in out),
        scratch_shapes=list(scratch),
        compiler_params=pltpu.CompilerParams(vmem_limit_bytes=limit * MIB),
        cost_estimate=pl.CostEstimate(flops=0, bytes_accessed=moved, transcendentals=0),
    )(*args)


def shaped(shape, dtype=jnp.bfloat16):
    return jax.ShapeDtypeStruct(shape, dtype)


def pack_body(offsets, ids, cot, own, for_core, across_a, across_b):
    mask = jnp.where(ids[...] != 0, 1.0, 0.0).astype(jnp.float32)
    wide = jnp.broadcast_to(mask, (B, B)).T
    half = across_a.shape[0] // 2

    def put(out, d, to, start, count):
        for i in range(count):
            column = pl.multiple_of(offsets[d, start + i] * B, B)
            out[to + i] = (cot[:, pl.ds(column, B)].astype(jnp.float32) * wide).astype(jnp.bfloat16)

    for d, to in ((2, 0), (3, half)):
        put(across_a, d, to, 0, half)
        put(across_b, d, to, half, half)
    put(own, 0, 0, 0, 2 * half)
    put(for_core, 1, 0, 0, 2 * half)


def norm_body(gain, *refs):
    count = (len(refs) - 2)
    normed, turned = refs[count:]
    blocks = normed.shape[0]
    for t in range(count):
        tok = refs[t]
        total = jnp.zeros((B, B), jnp.float32)
        for f in range(blocks):
            part = tok[:, f * B : (f + 1) * B].astype(jnp.float32)
            total = total + part * part
        mean = jnp.sum(total, axis=1, keepdims=True) * (1.0 / (blocks * B))
        inv = lax.rsqrt(mean + EPS)
        for f in range(blocks):
            part = tok[:, f * B : (f + 1) * B].astype(jnp.float32)
            scaled = part * inv * gain[:, f * B : (f + 1) * B].astype(jnp.float32)
            normed[f, t * B : (t + 1) * B, :] = scaled.astype(jnp.bfloat16)
            turned[f, :, t * B : (t + 1) * B] = scaled.T.astype(jnp.bfloat16)


class Rows:
    def __init__(self, lists, offsets):
        self.lists, self.offsets, self.slots = lists, offsets, lists.shape[0]

    def __getitem__(self, jm):
        j, m = jm
        return self.lists[m, self.offsets[0, j]]


def picked(ref, rows, j):
    return [ref[rows[j, m]] for m in range(rows.slots)]


def forward_block(rows, normed, cots, weight, j, scale):
    left = jnp.concatenate(picked(normed, rows, j), axis=1)
    pre = jnp.dot(left, weight, preferred_element_type=jnp.float32) * scale
    cot = jnp.concatenate(cots, axis=0).astype(jnp.float32)
    sig = jax.nn.sigmoid(pre)
    return (cot * (sig * (1.0 + pre * (1.0 - sig)))).astype(jnp.bfloat16)


def back_block(rows, acc, grad, weight, j):
    out = lax.dot_general(grad, weight, (((1,), (1,)), ((), ())), preferred_element_type=jnp.float32)
    for m in range(rows.slots):
        f = rows[j, m]
        acc[f] = acc[f] + out[:, m * B : (m + 1) * B]


def near_body(scale, lists, offsets, normed, own, got, w0, w2, w1, w3, grads, mine, theirs, acc):
    acc[...] = jnp.zeros_like(acc)
    rows = Rows(lists, offsets)
    per = w0.shape[0]

    def step(r, _):
        done = []
        for g, weights in enumerate((w0, w2, w1, w3)):
            j = g * per + r
            grad = forward_block(rows, normed, (own[j], got[j]), weights[r], j, scale)
            grads[j] = grad
            done.append((grad, weights, j))
        for grad, weights, j in done:
            back_block(rows, acc, grad, weights[r], j)
        return 0

    lax.fori_loop(0, per, step, 0)
    mine[...] = acc[:, :B, :] * scale
    theirs[...] = (acc[:, B:, :] * scale).astype(jnp.bfloat16)


def far_steps(scale, base, rows, normed, cots, more, pair, grads, acc):
    per = pair[0].shape[0]
    half = 2 * per

    def step(r, _):
        done = []
        for g, weights in enumerate(pair):
            i = g * per + r
            grad = forward_block(rows, normed, (cots[i], more[half + i]), weights[r], base + i, scale)
            grads[i] = grad
            done.append((grad, weights, base + i))
        for grad, weights, j in done:
            back_block(rows, acc, grad, weights[r], j)
        return 0

    lax.fori_loop(0, per, step, 0)


def far_first_body(scale, lists, offsets, normed, cots, more, w0, w2, grads, acc):
    acc[...] = jnp.zeros_like(acc)
    far_steps(scale, 0, Rows(lists, offsets), normed, cots, more, (w0, w2), grads, acc)


def far_second_body(scale, base, lists, offsets, normed, cots, more, before, w1, w3, grads, kept, passed, acc):
    acc[...] = before[...]
    far_steps(scale, base, Rows(lists, offsets), normed, cots, more, (w1, w3), grads, acc)
    kept[...] = acc[:, :B, :] * scale
    passed[...] = (acc[:, B:, :] * scale).astype(jnp.bfloat16)


def weight_body(scale, base, lists, offsets, near_turned, far_turned, near_grads, far_grads, out_a, out_b):
    per = out_a.shape[0]
    rows = Rows(lists, offsets)

    def step(r, _):
        for g, out in enumerate((out_a, out_b)):
            i = g * per + r
            j = base + i
            near = jnp.concatenate(picked(near_turned, rows, j), axis=0)
            far = jnp.concatenate(picked(far_turned, rows, j), axis=0)
            total = jnp.dot(near, near_grads[j], preferred_element_type=jnp.float32)
            total = total + jnp.dot(far, far_grads[i], preferred_element_type=jnp.float32)
            out[r] = (total * scale).astype(jnp.bfloat16)
        return 0

    lax.fori_loop(0, per, step, 0)


def sum_body(kept, passed, out):
    out[...] = (kept[...] + passed[...].astype(jnp.float32)).astype(jnp.bfloat16)


def update_body(weights, partner_w, momentum, partner_m, g0, g1, g2, g3, new_weights, new_momentum):
    f32 = jnp.float32
    weight_grad = g0[...].astype(f32) + g1[...].astype(f32) + g2[...].astype(f32) + g3[...].astype(f32)
    mean_moment = (momentum[...].astype(f32) + partner_m[...].astype(f32)) * 0.5
    mean_weights = (weights[...].astype(f32) + partner_w[...].astype(f32)) * 0.5
    moment_sum = 0.9 * mean_moment + weight_grad
    new_momentum[...] = moment_sum.astype(jnp.bfloat16)
    new_weights[...] = (mean_weights - 0.05 * moment_sum).astype(jnp.bfloat16)


def final_body(gain, tok, mine, core_part, far_part, out):
    blocks = mine.shape[0]
    total = jnp.zeros((B, B), jnp.float32)
    cross = jnp.zeros((B, B), jnp.float32)
    for f in range(blocks):
        part = tok[:, f * B : (f + 1) * B].astype(jnp.float32)
        total = total + part * part
        grad = mine[f] + core_part[f].astype(jnp.float32) + far_part[f].astype(jnp.float32)
        grad = grad * gain[:, f * B : (f + 1) * B].astype(jnp.float32)
        mine[f] = grad
        cross = cross + part * grad
    inv = lax.rsqrt(jnp.sum(total, axis=1, keepdims=True) * (1.0 / (blocks * B)) + EPS)
    mean = jnp.sum(cross, axis=1, keepdims=True) * (1.0 / (blocks * B))
    slope = inv * inv * inv * mean
    for f in range(blocks):
        part = tok[:, f * B : (f + 1) * B].astype(jnp.float32)
        out[:, f * B : (f + 1) * B] = (inv * mine[f] - part * slope).astype(jnp.bfloat16)


def final_entry(gain, tok, mine, core_part, far_part, out, kept):
    kept[...] = mine[...]
    final_body(gain, tok, kept, core_part, far_part, out)


def after(value, *earlier):
    return lax.optimization_barrier((value, earlier))[0]


def grouped(valid, work, *values):
    shapes = jax.eval_shape(work, *values)
    empty = lambda *_: jax.tree.map(lambda a: jnp.zeros(a.shape, a.dtype), shapes)
    return lax.cond(valid, work, empty, *values)


def per_device(tokens, norm_gain, cotangent, token_ids, step_index, block_rows, weights, momentum):
    gain, ids = norm_gain[None, :], token_ids[None, :]
    weights, momentum = weights[0], momentum[0]
    blocks = tokens.shape[1] // B
    per, slots = weights.shape[0], weights.shape[1]
    scale = float(slots * B) ** -0.5
    size = lax.axis_size("shard")
    ring = size // 4
    me = lax.axis_index("shard")
    y, q = me // 4, me % 4
    count = lax.axis_size("rep")
    levels = count.bit_length() - 1

    def hop(value, flip):
        return lax.ppermute(value, "shard", [(s, s ^ flip) for s in range(size)])

    def along(value, steps):
        return lax.ppermute(value, "shard", [(s, (s + 4 * steps) % size) for s in range(size)])

    def rep(exponent, value):
        return lax.ppermute(value, "rep", [(s, (s + 2**exponent) % count) for s in range(count)])

    def beside(exponent, work, value, *values):
        return rep(exponent, value), work(*values)

    def with_partner(work, value, *values):
        branches = [functools.partial(beside, e, work) for e in range(levels)]
        return lax.switch(step_index[0] % levels, branches, value, *values)

    order = (0, 2, 1, 3)
    owners = jnp.stack([(y + dy) % ring for dy in order])
    first = (owners[:, None] * (4 * per) + jnp.arange(per)[None, :]).reshape(-1)
    half = 2 * per
    full = 2 * half
    offsets = jnp.stack([first + (q ^ d) * per for d in range(4)])
    lists = block_rows.T
    acc = shaped((blocks, 2 * B, B), jnp.float32)
    scratch = [pltpu.VMEM(acc.shape, acc.dtype)]
    sums = [shaped((blocks, B, B), jnp.float32), shaped((blocks, B, B))]
    both = [shaped((blocks, 2 * B, B)), shaped((blocks, B, 2 * B))]
    terms = [shaped((per, slots * B, B))] * 2
    grads = shaped((half, 2 * B, B))
    piece = shaped((full, B, B))

    def opening(tokens, cotangent):
        tok_core = hop(tokens, 1)
        own, for_core, send_a, send_b = call(pack_body, [piece] * 4, (offsets, ids, cotangent), n_smem=1)
        got = hop(after(for_core, tok_core), 1)
        near, near_turned = call(norm_body, both, (gain, tokens, tok_core))
        return own, got, send_a, send_b, near, near_turned

    tok_far = hop(tokens, 2)
    w1, w3, w2 = along(weights, -1), along(weights, -3), along(weights, -2)
    own, got, send_a, send_b, near, near_turned = grouped(step_index[0] >= 0, opening, tokens, cotangent)
    cots_a = hop(send_a, 2)
    tok_far, near = after((tok_far, near), near_turned)
    (tok_diag,) = grouped(step_index[0] >= 0, lambda t: (hop(t, 1),), tok_far)

    def norm_work(gain, tok_far, tok_diag):
        return call(norm_body, both, (gain, tok_far, tok_diag))

    partner_w, (far, far_turned) = with_partner(norm_work, after(weights, tok_diag), gain, tok_far, tok_diag)
    w1, w3, w2, near = after((w1, w3, w2, near), (partner_w, far))
    cots_b = hop(after(send_b, far), 2)
    flat = [v.reshape(per, slots * B, B) for v in (weights, w2, w1, w3)]
    (more_a,) = grouped(step_index[0] >= 0, lambda t: (hop(t, 1),), after(cots_a, near))

    def middle(near, own, got, far, far_turned, near_turned, cots_a, more_a, *flat):
        near_grads, mine, theirs = call(
            functools.partial(near_body, scale),
            [shaped((full, 2 * B, B)), *sums],
            (lists, offsets, near, own, got, *flat),
            n_smem=2,
            scratch=scratch,
        )
        far_a, running = call(
            functools.partial(far_first_body, scale),
            [grads, acc],
            (lists, offsets, far, cots_a, more_a, *flat[:2]),
            n_smem=2,
        )
        g0, g2 = call(
            functools.partial(weight_body, scale, 0),
            terms,
            (lists, offsets, near_turned, far_turned, near_grads, far_a),
            n_smem=2,
        )
        return near_grads, mine, theirs, running, g0, g2

    partner_m, (near_grads, mine, theirs, running, g0, g2) = with_partner(
        middle, after(momentum, more_a), near, own, got, far, far_turned, near_turned, cots_a, more_a, *flat
    )
    got2 = along(g2, 2)

    def relays(cots_b, theirs):
        return hop(cots_b, 1), hop(theirs, 1)

    more_b, core_part = grouped(step_index[0] >= 0, relays, after(cots_b, g0), theirs)
    far_b, kept, passed = call(
        functools.partial(far_second_body, scale, half),
        [grads, *sums],
        (lists, offsets, far, cots_b, more_b, after(running, g0), *flat[2:]),
        n_smem=2,
        scratch=scratch,
    )
    g1, g3 = call(
        functools.partial(weight_body, scale, half),
        terms,
        (lists, offsets, near_turned, far_turned, near_grads, far_b),
        n_smem=2,
    )
    got1, got3 = along(g1, 1), along(g3, 3)

    from_core = hop(passed, 1)
    (summed,) = call(sum_body, [shaped(kept.shape)], (after(kept, (g1, g3, got2)), from_core))
    far_part = hop(summed, 2)
    (grad_tokens,) = call(
        final_entry,
        [shaped(tokens.shape)],
        (gain, after(tokens, got2), mine, core_part, far_part),
        moved=20 * MIB,
        scratch=[pltpu.VMEM((blocks, B, B), jnp.float32)],
    )
    rows = (per * slots * B, B)
    parts = (weights, partner_w, momentum, partner_m, g0, got1, got2, got3)
    new_weights, new_momentum = call(update_body, [shaped(rows)] * 2, tuple(v.reshape(rows) for v in parts))
    shape = (1, *weights.shape)
    return grad_tokens, new_weights.reshape(shape), new_momentum.reshape(shape)


def solution(mesh):
    placed = (
        P(("rep", "shard"), None),
        P(),
        P(("rep", "shard"), None),
        P(("rep", "shard")),
        P(),
        P(),
        P("rep", "shard", None, None, None),
        P("rep", "shard", None, None, None),
    )
    return jax.shard_map(
        per_device,
        mesh=mesh,
        in_specs=placed,
        out_specs=(
            P(("rep", "shard"), None),
            P("rep", "shard", None, None, None),
            P("rep", "shard", None, None, None),
        ),
        check_vma=False,
    )
```

```python
import functools

import jax
import jax.numpy as jnp
from jax import lax
from jax.experimental import pallas as pl
from jax.experimental.pallas import tpu as pltpu
from jax.sharding import PartitionSpec as P

B = 128
EPS = 1e-05
MIB = 1 << 20
VMEM = pl.BlockSpec(memory_space=pltpu.VMEM)
SMEM = pl.BlockSpec(memory_space=pltpu.SMEM)


def call(body, out, args, n_smem=0, scratch=(), limit=60, moved=0):
    return pl.pallas_call(
        body,
        out_shape=tuple(out),
        in_specs=[SMEM] * n_smem + [VMEM] * (len(args) - n_smem),
        out_specs=tuple(VMEM for _ in out),
        scratch_shapes=list(scratch),
        compiler_params=pltpu.CompilerParams(vmem_limit_bytes=limit * MIB),
        cost_estimate=pl.CostEstimate(flops=0, bytes_accessed=moved, transcendentals=0),
    )(*args)


def shaped(shape, dtype=jnp.bfloat16):
    return jax.ShapeDtypeStruct(shape, dtype)


def pack_body(offsets, ids, cot, own, for_core, across_a, across_b):
    mask = jnp.where(ids[...] != 0, 1.0, 0.0).astype(jnp.float32)
    wide = jnp.broadcast_to(mask, (B, B)).T
    half = across_a.shape[0] // 2

    def put(out, d, to, start, count):
        for i in range(count):
            column = pl.multiple_of(offsets[d, start + i] * B, B)
            out[to + i] = (cot[:, pl.ds(column, B)].astype(jnp.float32) * wide).astype(jnp.bfloat16)

    for d, to in ((2, 0), (3, half)):
        put(across_a, d, to, 0, half)
        put(across_b, d, to, half, half)
    put(own, 0, 0, 0, 2 * half)
    put(for_core, 1, 0, 0, 2 * half)


def norm_body(gain, *refs):
    count = (len(refs) - 2)
    normed, turned = refs[count:]
    blocks = normed.shape[0]
    for t in range(count):
        tok = refs[t]
        total = jnp.zeros((B, B), jnp.float32)
        for f in range(blocks):
            part = tok[:, f * B : (f + 1) * B].astype(jnp.float32)
            total = total + part * part
        mean = jnp.sum(total, axis=1, keepdims=True) * (1.0 / (blocks * B))
        inv = lax.rsqrt(mean + EPS)
        for f in range(blocks):
            part = tok[:, f * B : (f + 1) * B].astype(jnp.float32)
            scaled = part * inv * gain[:, f * B : (f + 1) * B].astype(jnp.float32)
            normed[f, t * B : (t + 1) * B, :] = scaled.astype(jnp.bfloat16)
            turned[f, :, t * B : (t + 1) * B] = scaled.T.astype(jnp.bfloat16)


class Rows:
    def __init__(self, lists, offsets):
        self.lists, self.offsets, self.slots = lists, offsets, lists.shape[0]

    def __getitem__(self, jm):
        j, m = jm
        return self.lists[m, self.offsets[0, j]]


def picked(ref, rows, j):
    return [ref[rows[j, m]] for m in range(rows.slots)]


def forward_block(rows, normed, cots, weight, j, scale):
    left = jnp.concatenate(picked(normed, rows, j), axis=1)
    pre = jnp.dot(left, weight, preferred_element_type=jnp.float32) * scale
    cot = jnp.concatenate(cots, axis=0).astype(jnp.float32)
    sig = jax.nn.sigmoid(pre)
    return (cot * (sig * (1.0 + pre * (1.0 - sig)))).astype(jnp.bfloat16)


def back_block(rows, acc, grad, weight, j):
    out = lax.dot_general(grad, weight, (((1,), (1,)), ((), ())), preferred_element_type=jnp.float32)
    for m in range(rows.slots):
        f = rows[j, m]
        acc[f] = acc[f] + out[:, m * B : (m + 1) * B]


def near_body(scale, lists, offsets, normed, own, got, w0, w2, w1, w3, grads, mine, theirs, acc):
    acc[...] = jnp.zeros_like(acc)
    rows = Rows(lists, offsets)
    per = w0.shape[0]

    def step(r, _):
        done = []
        for g, weights in enumerate((w0, w2, w1, w3)):
            j = g * per + r
            grad = forward_block(rows, normed, (own[j], got[j]), weights[r], j, scale)
            grads[j] = grad
            done.append((grad, weights, j))
        for grad, weights, j in done:
            back_block(rows, acc, grad, weights[r], j)
        return 0

    lax.fori_loop(0, per, step, 0)
    mine[...] = acc[:, :B, :] * scale
    theirs[...] = (acc[:, B:, :] * scale).astype(jnp.bfloat16)


def far_steps(scale, base, rows, normed, cots, more, pair, grads, acc):
    per = pair[0].shape[0]
    half = 2 * per

    def step(r, _):
        done = []
        for g, weights in enumerate(pair):
            i = g * per + r
            grad = forward_block(rows, normed, (cots[i], more[half + i]), weights[r], base + i, scale)
            grads[i] = grad
            done.append((grad, weights, base + i))
        for grad, weights, j in done:
            back_block(rows, acc, grad, weights[r], j)
        return 0

    lax.fori_loop(0, per, step, 0)


def far_first_body(scale, lists, offsets, normed, cots, more, w0, w2, grads, acc):
    acc[...] = jnp.zeros_like(acc)
    far_steps(scale, 0, Rows(lists, offsets), normed, cots, more, (w0, w2), grads, acc)


def far_second_body(scale, base, lists, offsets, normed, cots, more, before, w1, w3, grads, kept, passed, acc):
    acc[...] = before[...]
    far_steps(scale, base, Rows(lists, offsets), normed, cots, more, (w1, w3), grads, acc)
    kept[...] = acc[:, :B, :] * scale
    passed[...] = (acc[:, B:, :] * scale).astype(jnp.bfloat16)


def weight_body(scale, base, lists, offsets, near_turned, far_turned, near_grads, far_grads, out_a, out_b):
    per = out_a.shape[0]
    rows = Rows(lists, offsets)

    def step(r, _):
        for g, out in enumerate((out_a, out_b)):
            i = g * per + r
            j = base + i
            near = jnp.concatenate(picked(near_turned, rows, j), axis=0)
            far = jnp.concatenate(picked(far_turned, rows, j), axis=0)
            total = jnp.dot(near, near_grads[j], preferred_element_type=jnp.float32)
            total = total + jnp.dot(far, far_grads[i], preferred_element_type=jnp.float32)
            out[r] = (total * scale).astype(jnp.bfloat16)
        return 0

    lax.fori_loop(0, per, step, 0)


def far_last_body(
    scale, base, lists, offsets, normed, cots, more, before, w1, w3, near_turned, far_turned, near_grads,
    kept, passed, out_a, out_b, acc, grads,
):
    far_second_body(scale, base, lists, offsets, normed, cots, more, before, w1, w3, grads, kept, passed, acc)
    weight_body(scale, base, lists, offsets, near_turned, far_turned, near_grads, grads, out_a, out_b)


def sum_body(kept, passed, out):
    out[...] = (kept[...] + passed[...].astype(jnp.float32)).astype(jnp.bfloat16)


def update_body(weights, partner_w, momentum, partner_m, g0, g1, g2, g3, new_weights, new_momentum):
    f32 = jnp.float32
    weight_grad = g0[...].astype(f32) + g1[...].astype(f32) + g2[...].astype(f32) + g3[...].astype(f32)
    mean_moment = (momentum[...].astype(f32) + partner_m[...].astype(f32)) * 0.5
    mean_weights = (weights[...].astype(f32) + partner_w[...].astype(f32)) * 0.5
    moment_sum = 0.9 * mean_moment + weight_grad
    new_momentum[...] = moment_sum.astype(jnp.bfloat16)
    new_weights[...] = (mean_weights - 0.05 * moment_sum).astype(jnp.bfloat16)


def final_body(gain, tok, mine, core_part, far_part, out):
    blocks = mine.shape[0]
    total = jnp.zeros((B, B), jnp.float32)
    cross = jnp.zeros((B, B), jnp.float32)
    for f in range(blocks):
        part = tok[:, f * B : (f + 1) * B].astype(jnp.float32)
        total = total + part * part
        grad = mine[f] + core_part[f].astype(jnp.float32) + far_part[f].astype(jnp.float32)
        grad = grad * gain[:, f * B : (f + 1) * B].astype(jnp.float32)
        mine[f] = grad
        cross = cross + part * grad
    inv = lax.rsqrt(jnp.sum(total, axis=1, keepdims=True) * (1.0 / (blocks * B)) + EPS)
    mean = jnp.sum(cross, axis=1, keepdims=True) * (1.0 / (blocks * B))
    slope = inv * inv * inv * mean
    for f in range(blocks):
        part = tok[:, f * B : (f + 1) * B].astype(jnp.float32)
        out[:, f * B : (f + 1) * B] = (inv * mine[f] - part * slope).astype(jnp.bfloat16)


def final_entry(gain, tok, mine, core_part, far_part, out, kept):
    kept[...] = mine[...]
    final_body(gain, tok, kept, core_part, far_part, out)


def after(value, *earlier):
    return lax.optimization_barrier((value, earlier))[0]


def grouped(valid, work, *values):
    shapes = jax.eval_shape(work, *values)
    empty = lambda *_: jax.tree.map(lambda a: jnp.zeros(a.shape, a.dtype), shapes)
    return lax.cond(valid, work, empty, *values)


def per_device(tokens, norm_gain, cotangent, token_ids, step_index, block_rows, weights, momentum):
    gain, ids = norm_gain[None, :], token_ids[None, :]
    weights, momentum = weights[0], momentum[0]
    blocks = tokens.shape[1] // B
    per, slots = weights.shape[0], weights.shape[1]
    scale = float(slots * B) ** -0.5
    size = lax.axis_size("shard")
    ring = size // 4
    me = lax.axis_index("shard")
    y, q = me // 4, me % 4
    count = lax.axis_size("rep")
    levels = count.bit_length() - 1

    def hop(value, flip):
        return lax.ppermute(value, "shard", [(s, s ^ flip) for s in range(size)])

    def along(value, steps):
        return lax.ppermute(value, "shard", [(s, (s + 4 * steps) % size) for s in range(size)])

    def rep(exponent, value):
        return lax.ppermute(value, "rep", [(s, (s + 2**exponent) % count) for s in range(count)])

    def beside(exponent, work, value, *values):
        return rep(exponent, value), work(*values)

    def with_partner(work, value, *values):
        branches = [functools.partial(beside, e, work) for e in range(levels)]
        return lax.switch(step_index[0] % levels, branches, value, *values)

    order = (0, 2, 1, 3)
    owners = jnp.stack([(y + dy) % ring for dy in order])
    first = (owners[:, None] * (4 * per) + jnp.arange(per)[None, :]).reshape(-1)
    half = 2 * per
    full = 2 * half
    offsets = jnp.stack([first + (q ^ d) * per for d in range(4)])
    lists = block_rows.T
    acc = shaped((blocks, 2 * B, B), jnp.float32)
    scratch = [pltpu.VMEM(acc.shape, acc.dtype)]
    sums = [shaped((blocks, B, B), jnp.float32), shaped((blocks, B, B))]
    both = [shaped((blocks, 2 * B, B)), shaped((blocks, B, 2 * B))]
    terms = [shaped((per, slots * B, B))] * 2
    grads = shaped((half, 2 * B, B))
    piece = shaped((full, B, B))

    def opening(tokens, cotangent):
        tok_core = hop(tokens, 1)
        own, for_core, send_a, send_b = call(pack_body, [piece] * 4, (offsets, ids, cotangent), n_smem=1)
        got = hop(after(for_core, tok_core), 1)
        near, near_turned = call(norm_body, both, (gain, tokens, tok_core))
        return own, got, send_a, send_b, near, near_turned

    tok_far = hop(tokens, 2)
    w1, w3, w2 = along(weights, -1), along(weights, -3), along(weights, -2)
    own, got, send_a, send_b, near, near_turned = grouped(step_index[0] >= 0, opening, tokens, cotangent)
    cots_a = hop(send_a, 2)
    tok_far, near = after((tok_far, near), near_turned)
    (tok_diag,) = grouped(step_index[0] >= 0, lambda t: (hop(t, 1),), tok_far)

    def norm_work(gain, tok_far, tok_diag):
        return call(norm_body, both, (gain, tok_far, tok_diag))

    partner_w, (far, far_turned) = with_partner(norm_work, after(weights, tok_diag), gain, tok_far, tok_diag)
    w1, w3, w2, near = after((w1, w3, w2, near), (partner_w, far))
    cots_b = hop(after(send_b, far), 2)
    flat = [v.reshape(per, slots * B, B) for v in (weights, w2, w1, w3)]
    (more_a,) = grouped(step_index[0] >= 0, lambda t: (hop(t, 1),), after(cots_a, near))

    def middle(near, own, got, far, far_turned, near_turned, cots_a, more_a, *flat):
        near_grads, mine, theirs = call(
            functools.partial(near_body, scale),
            [shaped((full, 2 * B, B)), *sums],
            (lists, offsets, near, own, got, *flat),
            n_smem=2,
            scratch=scratch,
        )
        far_a, running = call(
            functools.partial(far_first_body, scale),
            [grads, acc],
            (lists, offsets, far, cots_a, more_a, *flat[:2]),
            n_smem=2,
        )
        g0, g2 = call(
            functools.partial(weight_body, scale, 0),
            terms,
            (lists, offsets, near_turned, far_turned, near_grads, far_a),
            n_smem=2,
        )
        return near_grads, mine, theirs, running, g0, g2

    partner_m, (near_grads, mine, theirs, running, g0, g2) = with_partner(
        middle, after(momentum, more_a), near, own, got, far, far_turned, near_turned, cots_a, more_a, *flat
    )
    got2 = along(g2, 2)

    def relays(cots_b, theirs):
        return hop(cots_b, 1), hop(theirs, 1)

    more_b, core_part = grouped(step_index[0] >= 0, relays, after(cots_b, g0), theirs)
    kept, passed, g1, g3 = call(
        functools.partial(far_last_body, scale, half),
        [*sums, *terms],
        (lists, offsets, far, cots_b, more_b, after(running, g0), *flat[2:], near_turned, far_turned, near_grads),
        n_smem=2,
        scratch=[*scratch, pltpu.VMEM(grads.shape, grads.dtype)],
    )
    from_core = hop(passed, 1)
    got1, got3 = along(g1, 1), along(g3, 3)

    (summed,) = call(sum_body, [shaped(kept.shape)], (after(kept, (g1, g3, got2)), from_core))
    far_part = hop(summed, 2)
    (grad_tokens,) = call(
        final_entry,
        [shaped(tokens.shape)],
        (gain, after(tokens, got2), mine, core_part, far_part),
        moved=20 * MIB,
        scratch=[pltpu.VMEM((blocks, B, B), jnp.float32)],
    )
    rows = (per * slots * B, B)
    parts = (weights, partner_w, momentum, partner_m, g0, got1, got2, got3)
    new_weights, new_momentum = call(update_body, [shaped(rows)] * 2, tuple(v.reshape(rows) for v in parts))
    shape = (1, *weights.shape)
    return grad_tokens, new_weights.reshape(shape), new_momentum.reshape(shape)


def solution(mesh):
    placed = (
        P(("rep", "shard"), None),
        P(),
        P(("rep", "shard"), None),
        P(("rep", "shard")),
        P(),
        P(),
        P("rep", "shard", None, None, None),
        P("rep", "shard", None, None, None),
    )
    return jax.shard_map(
        per_device,
        mesh=mesh,
        in_specs=placed,
        out_specs=(
            P(("rep", "shard"), None),
            P("rep", "shard", None, None, None),
            P("rep", "shard", None, None, None),
        ),
        check_vma=False,
    )
```

```python
import functools

import jax
import jax.numpy as jnp
from jax import lax
from jax.experimental import pallas as pl
from jax.experimental.pallas import tpu as pltpu
from jax.sharding import PartitionSpec as P

B = 128
EPS = 1e-05
MIB = 1 << 20
VMEM = pl.BlockSpec(memory_space=pltpu.VMEM)
SMEM = pl.BlockSpec(memory_space=pltpu.SMEM)


def call(body, out, args, n_smem=0, scratch=(), limit=60, moved=0):
    return pl.pallas_call(
        body,
        out_shape=tuple(out),
        in_specs=[SMEM] * n_smem + [VMEM] * (len(args) - n_smem),
        out_specs=tuple(VMEM for _ in out),
        scratch_shapes=list(scratch),
        compiler_params=pltpu.CompilerParams(vmem_limit_bytes=limit * MIB),
        cost_estimate=pl.CostEstimate(flops=0, bytes_accessed=moved, transcendentals=0),
    )(*args)


def shaped(shape, dtype=jnp.bfloat16):
    return jax.ShapeDtypeStruct(shape, dtype)


def pack_body(offsets, ids, cot, own, for_core, across_a, across_b):
    mask = jnp.where(ids[...] != 0, 1.0, 0.0).astype(jnp.float32)
    wide = jnp.broadcast_to(mask, (B, B)).T
    half = across_a.shape[0] // 2

    def put(out, d, to, start, count):
        for i in range(count):
            column = pl.multiple_of(offsets[d, start + i] * B, B)
            out[to + i] = (cot[:, pl.ds(column, B)].astype(jnp.float32) * wide).astype(jnp.bfloat16)

    for d, to in ((2, 0), (3, half)):
        put(across_a, d, to, 0, half)
        put(across_b, d, to, half, half)
    put(own, 0, 0, 0, 2 * half)
    put(for_core, 1, 0, 0, 2 * half)


def norm_body(gain, *refs):
    count = (len(refs) - 2)
    normed, turned = refs[count:]
    blocks = normed.shape[0]
    for t in range(count):
        tok = refs[t]
        total = jnp.zeros((B, B), jnp.float32)
        for f in range(blocks):
            part = tok[:, f * B : (f + 1) * B].astype(jnp.float32)
            total = total + part * part
        mean = jnp.sum(total, axis=1, keepdims=True) * (1.0 / (blocks * B))
        inv = lax.rsqrt(mean + EPS)
        for f in range(blocks):
            part = tok[:, f * B : (f + 1) * B].astype(jnp.float32)
            scaled = part * inv * gain[:, f * B : (f + 1) * B].astype(jnp.float32)
            normed[f, t * B : (t + 1) * B, :] = scaled.astype(jnp.bfloat16)
            turned[f, :, t * B : (t + 1) * B] = scaled.T.astype(jnp.bfloat16)


class Rows:
    def __init__(self, lists, offsets):
        self.lists, self.offsets, self.slots = lists, offsets, lists.shape[0]

    def __getitem__(self, jm):
        j, m = jm
        return self.lists[m, self.offsets[0, j]]


def picked(ref, rows, j):
    return [ref[rows[j, m]] for m in range(rows.slots)]


def forward_block(rows, normed, cots, weight, j, scale):
    left = jnp.concatenate(picked(normed, rows, j), axis=1)
    pre = jnp.dot(left, weight, preferred_element_type=jnp.float32) * scale
    cot = jnp.concatenate(cots, axis=0).astype(jnp.float32)
    sig = jax.nn.sigmoid(pre)
    return (cot * (sig * (1.0 + pre * (1.0 - sig)))).astype(jnp.bfloat16)


def back_block(rows, acc, grad, weight, j):
    out = lax.dot_general(grad, weight, (((1,), (1,)), ((), ())), preferred_element_type=jnp.float32)
    for m in range(rows.slots):
        f = rows[j, m]
        acc[f] = acc[f] + out[:, m * B : (m + 1) * B]


def near_body(scale, lists, offsets, normed, own, got, w0, w2, w1, w3, grads, mine, theirs, acc):
    acc[...] = jnp.zeros_like(acc)
    rows = Rows(lists, offsets)
    per = w0.shape[0]

    def step(r, _):
        done = []
        for g, weights in enumerate((w0, w2, w1, w3)):
            j = g * per + r
            grad = forward_block(rows, normed, (own[j], got[j]), weights[r], j, scale)
            grads[j] = grad
            done.append((grad, weights, j))
        for grad, weights, j in done:
            back_block(rows, acc, grad, weights[r], j)
        return 0

    lax.fori_loop(0, per, step, 0)
    mine[...] = acc[:, :B, :] * scale
    theirs[...] = (acc[:, B:, :] * scale).astype(jnp.bfloat16)


def far_steps(scale, base, rows, normed, cots, more, pair, grads, acc):
    per = pair[0].shape[0]
    half = 2 * per

    def step(r, _):
        done = []
        for g, weights in enumerate(pair):
            i = g * per + r
            grad = forward_block(rows, normed, (cots[i], more[half + i]), weights[r], base + i, scale)
            grads[i] = grad
            done.append((grad, weights, base + i))
        for grad, weights, j in done:
            back_block(rows, acc, grad, weights[r], j)
        return 0

    lax.fori_loop(0, per, step, 0)


def far_first_body(scale, lists, offsets, normed, cots, more, w0, w2, grads, acc):
    acc[...] = jnp.zeros_like(acc)
    far_steps(scale, 0, Rows(lists, offsets), normed, cots, more, (w0, w2), grads, acc)


def far_second_body(scale, base, lists, offsets, normed, cots, more, before, w1, w3, grads, kept, passed, acc):
    acc[...] = before[...]
    far_steps(scale, base, Rows(lists, offsets), normed, cots, more, (w1, w3), grads, acc)
    kept[...] = acc[:, :B, :] * scale
    passed[...] = (acc[:, B:, :] * scale).astype(jnp.bfloat16)


def weight_body(scale, base, lists, offsets, near_turned, far_turned, near_grads, far_grads, out_a, out_b):
    per = out_a.shape[0]
    rows = Rows(lists, offsets)

    def step(r, _):
        for g, out in enumerate((out_a, out_b)):
            i = g * per + r
            j = base + i
            near = jnp.concatenate(picked(near_turned, rows, j), axis=0)
            far = jnp.concatenate(picked(far_turned, rows, j), axis=0)
            total = jnp.dot(near, near_grads[j], preferred_element_type=jnp.float32)
            total = total + jnp.dot(far, far_grads[i], preferred_element_type=jnp.float32)
            out[r] = (total * scale).astype(jnp.bfloat16)
        return 0

    lax.fori_loop(0, per, step, 0)


def far_last_body(
    scale, base, lists, offsets, normed, cots, more, before, w1, w3, near_turned, far_turned, near_grads,
    kept, passed, out_a, out_b, acc, grads,
):
    far_second_body(scale, base, lists, offsets, normed, cots, more, before, w1, w3, grads, kept, passed, acc)
    weight_body(scale, base, lists, offsets, near_turned, far_turned, near_grads, grads, out_a, out_b)


def sum_body(kept, passed, out):
    out[...] = (kept[...] + passed[...].astype(jnp.float32)).astype(jnp.bfloat16)


def update_body(weights, partner_w, momentum, partner_m, g0, g1, g2, g3, new_weights, new_momentum):
    f32 = jnp.float32
    weight_grad = g0[...].astype(f32) + g1[...].astype(f32) + g2[...].astype(f32) + g3[...].astype(f32)
    mean_moment = (momentum[...].astype(f32) + partner_m[...].astype(f32)) * 0.5
    mean_weights = (weights[...].astype(f32) + partner_w[...].astype(f32)) * 0.5
    moment_sum = 0.9 * mean_moment + weight_grad
    new_momentum[...] = moment_sum.astype(jnp.bfloat16)
    new_weights[...] = (mean_weights - 0.05 * moment_sum).astype(jnp.bfloat16)


def final_body(gain, tok, mine, core_part, far_part, out):
    blocks = mine.shape[0]
    total = jnp.zeros((B, B), jnp.float32)
    cross = jnp.zeros((B, B), jnp.float32)
    for f in range(blocks):
        part = tok[:, f * B : (f + 1) * B].astype(jnp.float32)
        total = total + part * part
        grad = mine[f] + core_part[f].astype(jnp.float32) + far_part[f].astype(jnp.float32)
        grad = grad * gain[:, f * B : (f + 1) * B].astype(jnp.float32)
        mine[f] = grad
        cross = cross + part * grad
    inv = lax.rsqrt(jnp.sum(total, axis=1, keepdims=True) * (1.0 / (blocks * B)) + EPS)
    mean = jnp.sum(cross, axis=1, keepdims=True) * (1.0 / (blocks * B))
    slope = inv * inv * inv * mean
    for f in range(blocks):
        part = tok[:, f * B : (f + 1) * B].astype(jnp.float32)
        out[:, f * B : (f + 1) * B] = (inv * mine[f] - part * slope).astype(jnp.bfloat16)


def final_entry(gain, tok, mine, core_part, far_part, out, kept):
    kept[...] = mine[...]
    final_body(gain, tok, kept, core_part, far_part, out)


def after(value, *earlier):
    return lax.optimization_barrier((value, earlier))[0]


def grouped(valid, work, *values):
    shapes = jax.eval_shape(work, *values)
    empty = lambda *_: jax.tree.map(lambda a: jnp.zeros(a.shape, a.dtype), shapes)
    return lax.cond(valid, work, empty, *values)


def per_device(tokens, norm_gain, cotangent, token_ids, step_index, block_rows, weights, momentum):
    gain, ids = norm_gain[None, :], token_ids[None, :]
    weights, momentum = weights[0], momentum[0]
    blocks = tokens.shape[1] // B
    per, slots = weights.shape[0], weights.shape[1]
    scale = float(slots * B) ** -0.5
    size = lax.axis_size("shard")
    ring = size // 4
    me = lax.axis_index("shard")
    y, q = me // 4, me % 4
    count = lax.axis_size("rep")
    levels = count.bit_length() - 1

    def hop(value, flip):
        return lax.ppermute(value, "shard", [(s, s ^ flip) for s in range(size)])

    def along(value, steps):
        return lax.ppermute(value, "shard", [(s, (s + 4 * steps) % size) for s in range(size)])

    def rep(exponent, value):
        return lax.ppermute(value, "rep", [(s, (s + 2**exponent) % count) for s in range(count)])

    def beside(exponent, work, value, *values):
        return rep(exponent, value), work(*values)

    def with_partner(work, value, *values):
        branches = [functools.partial(beside, e, work) for e in range(levels)]
        return lax.switch(step_index[0] % levels, branches, value, *values)

    order = (0, 2, 1, 3)
    owners = jnp.stack([(y + dy) % ring for dy in order])
    first = (owners[:, None] * (4 * per) + jnp.arange(per)[None, :]).reshape(-1)
    half = 2 * per
    full = 2 * half
    offsets = jnp.stack([first + (q ^ d) * per for d in range(4)])
    lists = block_rows.T
    acc = shaped((blocks, 2 * B, B), jnp.float32)
    scratch = [pltpu.VMEM(acc.shape, acc.dtype)]
    sums = [shaped((blocks, B, B), jnp.float32), shaped((blocks, B, B))]
    both = [shaped((blocks, 2 * B, B)), shaped((blocks, B, 2 * B))]
    terms = [shaped((per, slots * B, B))] * 2
    grads = shaped((half, 2 * B, B))
    piece = shaped((full, B, B))

    def opening(tokens, cotangent):
        tok_core = hop(tokens, 1)
        own, for_core, send_a, send_b = call(pack_body, [piece] * 4, (offsets, ids, cotangent), n_smem=1)
        got = hop(after(for_core, tok_core), 1)
        near, near_turned = call(norm_body, both, (gain, tokens, tok_core))
        return own, got, send_a, send_b, near, near_turned

    tok_far = hop(tokens, 2)
    w1, w3, w2 = along(weights, -1), along(weights, -3), along(weights, -2)
    own, got, send_a, send_b, near, near_turned = grouped(step_index[0] >= 0, opening, tokens, cotangent)
    cots_a = hop(send_a, 2)
    tok_far, near = after((tok_far, near), near_turned)
    (tok_diag,) = grouped(step_index[0] >= 0, lambda t: (hop(t, 1),), tok_far)

    def norm_work(gain, tok_far, tok_diag):
        return call(norm_body, both, (gain, tok_far, tok_diag))

    partner_w, (far, far_turned) = with_partner(norm_work, after(weights, tok_diag), gain, tok_far, tok_diag)
    w1, w3, w2, near = after((w1, w3, w2, near), (partner_w, far))
    cots_b = hop(after(send_b, far), 2)
    flat = [v.reshape(per, slots * B, B) for v in (weights, w2, w1, w3)]
    (more_a,) = grouped(step_index[0] >= 0, lambda t: (hop(t, 1),), after(cots_a, near))

    def middle(near, own, got, far, far_turned, near_turned, cots_a, more_a, *flat):
        near_grads, mine, theirs = call(
            functools.partial(near_body, scale),
            [shaped((full, 2 * B, B)), *sums],
            (lists, offsets, near, own, got, *flat),
            n_smem=2,
            scratch=scratch,
        )
        far_a, running = call(
            functools.partial(far_first_body, scale),
            [grads, acc],
            (lists, offsets, far, cots_a, more_a, *flat[:2]),
            n_smem=2,
        )
        g0, g2 = call(
            functools.partial(weight_body, scale, 0),
            terms,
            (lists, offsets, near_turned, far_turned, near_grads, far_a),
            n_smem=2,
        )
        return near_grads, mine, theirs, running, g0, g2

    partner_m, (near_grads, mine, theirs, running, g0, g2) = with_partner(
        middle, after(momentum, more_a), near, own, got, far, far_turned, near_turned, cots_a, more_a, *flat
    )
    got2 = along(g2, 2)

    def relays(cots_b, theirs):
        return hop(cots_b, 1), hop(theirs, 1)

    more_b, core_part = grouped(step_index[0] >= 0, relays, after(cots_b, g0), theirs)
    kept, passed, g1, g3 = call(
        functools.partial(far_last_body, scale, half),
        [*sums, *terms],
        (lists, offsets, far, cots_b, more_b, after(running, g0), *flat[2:], near_turned, far_turned, near_grads),
        n_smem=2,
        scratch=[*scratch, pltpu.VMEM(grads.shape, grads.dtype)],
    )
    from_core = hop(passed, 1)
    got1, got3 = along(g1, 1), along(g3, 3)

    (summed,) = call(sum_body, [shaped(kept.shape)], (after(kept, (g1, g3, got2)), from_core), limit=16)
    far_part = hop(summed, 2)
    (grad_tokens,) = call(
        final_entry,
        [shaped(tokens.shape)],
        (gain, after(tokens, got2), mine, core_part, far_part),
        moved=20 * MIB,
        limit=16,
        scratch=[pltpu.VMEM((blocks, B, B), jnp.float32)],
    )
    rows = (per * slots * B, B)
    parts = (weights, partner_w, momentum, partner_m, g0, got1, got2, got3)
    new_weights, new_momentum = call(update_body, [shaped(rows)] * 2, tuple(v.reshape(rows) for v in parts), limit=16)
    shape = (1, *weights.shape)
    return grad_tokens, new_weights.reshape(shape), new_momentum.reshape(shape)


def solution(mesh):
    placed = (
        P(("rep", "shard"), None),
        P(),
        P(("rep", "shard"), None),
        P(("rep", "shard")),
        P(),
        P(),
        P("rep", "shard", None, None, None),
        P("rep", "shard", None, None, None),
    )
    return jax.shard_map(
        per_device,
        mesh=mesh,
        in_specs=placed,
        out_specs=(
            P(("rep", "shard"), None),
            P("rep", "shard", None, None, None),
            P("rep", "shard", None, None, None),
        ),
        check_vma=False,
    )
```
